512 devices in a mesh: rep: 32 (over z, y_hi, core), fsdp: 16 (over x, y_lo).
Axes of the slice: x: 4, y: 8 (y_hi: 2, y_lo: 4; y = y_hi * 4 + y_lo), z: 8, core: 2. Of those that a mesh axis runs over, the one named last changes fastest.
Arguments:
- tokens: bfloat16 [131072, 4096], P(('rep', 'fsdp')), may hold values from -6 to 6
- cotangent: bfloat16 [131072, 512], P(('rep', 'fsdp')), may hold values from -6 to 6
- norm_gain: float32 [4096], replicated, may hold values from 0.25 to 1.75
- local_weight: bfloat16 [32, 4096, 512], P('rep', 'fsdp'), may hold values from -0.1875 to 0.1875
- anchor_weight: bfloat16 [4096, 512], P('fsdp'), may hold values from -0.09375 to 0.09375
- outer_master: float32 [4096, 512], P(('fsdp', 'rep')), may hold values from -0.09375 to 0.09375
- outer_moment: float32 [4096, 512], P(('fsdp', 'rep')), may hold values from -0.06 to 0.06
Outputs:
- grad_weight: bfloat16 [32, 4096, 512], P('rep', 'fsdp')
- grad_tokens: bfloat16 [131072, 4096], P(('rep', 'fsdp'))
- synced_weight: bfloat16 [4096, 512], P('fsdp')
- new_master: float32 [4096, 512], P(('fsdp', 'rep'))
- new_moment: float32 [4096, 512], P(('fsdp', 'rep'))
The draws below stay inside these ranges and needn't reach their ends.
All inputs are finite; a program needn't handle non-finite values.
Results may differ from the reference program's by a relative error of at most 0.03.
Values may be sent and summed in bfloat16 or wider, within the bound.
No kernel may reach another device: no remote copies, remote signals or barrier semaphores. Data moves between devices by JAX's collectives and lax.ppermute only.
A program may use at most 64 MiB of HBM per device.

```python
import jax
import jax.numpy as jnp
from jax import lax

D = 4096
KV = 512
TOK_DEV = 256
REPLICAS = 32
TOKENS = 131072
N_REP = 32
N_FSDP = 16


def strengthened(entries, key, source, target, blocks, factor):
    owner, partner = [(jnp.arange(entries.shape[position]) // (entries.shape[position] // blocks)).reshape([-1 if axis == position else 1 for axis in range(entries.ndim)]) for position in (source, target)]
    chosen = jax.random.permutation(key, blocks)[partner]
    strong = (owner == chosen) | (owner == (partner + blocks // 2) % blocks)
    return jnp.where(strong, factor * entries, entries)


def steps_of(stream_key, shape, pieces, smallest, top_value):
    factor_of, own = 1.0, jax.random.fold_in(stream_key, 6)
    for dim, parts in pieces:
        draws = jnp.exp(jax.random.uniform(jax.random.fold_in(own, dim), (parts,), jnp.float32, smallest / len(pieces), top_value / len(pieces)))
        factor_of = factor_of * jnp.repeat(draws, shape[dim] // parts).reshape([-1 if axis == dim else 1 for axis in range(len(shape))])
    return factor_of


def noise(own_key, shape, spread, bound, split=(), dtype=jnp.bfloat16):
    factor_of = steps_of(own_key, shape, split, -0.22, 0.18) if split else 1.0
    entries = jax.random.normal(own_key, shape, jnp.float32) * spread * factor_of
    return jnp.minimum(jnp.maximum(entries, -bound), bound).astype(dtype)


def gaussian_with(rng, dims, deviation, reach, shards, heavy, held_as=jnp.bfloat16):
    drawn = deviation * jax.random.normal(rng, dims, jnp.float32)
    if shards:
        drawn = drawn * steps_of(rng, dims, shards, -0.22, 0.18)
    return jnp.clip(strengthened(drawn, jax.random.fold_in(rng, 3), *heavy), -reach, reach).astype(held_as)


def setup_inputs(seed: int = 0) -> dict:
    streams_of = jax.random.split(jax.random.key(seed), 8)
    return {
        "tokens": noise(streams_of[0], (TOKENS, D), 1.0, 6.0, ((0, 512),)),
        "cotangent": noise(streams_of[1], (TOKENS, KV), 1.0, 6.0, ((0, 512),)),
        "norm_gain": jnp.clip(1.0 + 0.15 * jax.random.normal(streams_of[2], (D,), jnp.float32), 0.25, 1.75),
        "local_weight": gaussian_with(streams_of[3], (REPLICAS, D, KV), D ** -0.5, 0.1875, ((0, 32), (1, 16)), (0, 1, 32, 2.75)),
        "anchor_weight": noise(streams_of[4], (D, KV), D ** -0.5, 0.09375, ((0, 16),)),
        "outer_master": noise(streams_of[5], (D, KV), D ** -0.5, 0.09375, ((0, 512),), jnp.float32),
        "outer_moment": noise(streams_of[6], (D, KV), 0.01, 0.06, ((0, 512),), jnp.float32),
    }


scale_eps = 1e-06
code_range = 448.0
norm_eps = 1e-05
outer_mu = 0.9
outer_rate = 0.7

def quantize(values):
    blocks = values.reshape(values.shape[:-1] + (values.shape[-1] // 128, 128))
    peak = lax.optimization_barrier(jnp.max(jnp.abs(blocks), axis=-1))
    scale = ((peak + scale_eps) / code_range).astype(jnp.bfloat16)
    codes = (blocks / scale.astype(jnp.float32)[..., None]).astype(jnp.bfloat16)
    return (codes.reshape(values.shape), scale)

def dequantize(codes, scale):
    blocks = codes.astype(jnp.float32).reshape(codes.shape[:-1] + (codes.shape[-1] // 128, 128))
    return (blocks * scale.astype(jnp.float32)[..., None]).reshape(codes.shape)

def reference(tokens, cotangent, norm_gain, local_weight, anchor_weight, outer_master, outer_moment):
    per_rep = tokens.reshape(N_REP, N_FSDP * TOK_DEV, D)
    cot_rep = cotangent.reshape(N_REP, N_FSDP * TOK_DEV, KV)

    def replica(item):
        inputs, cot, weight = item
        xfull = inputs.astype(jnp.float32)
        inv = lax.rsqrt(lax.optimization_barrier(jnp.mean(xfull * xfull, axis=-1, keepdims=True)) + norm_eps)
        normed = (xfull * inv * norm_gain).astype(jnp.bfloat16)
        groups_n = normed.reshape(N_FSDP, TOK_DEV, D)
        groups_c = cot.reshape(N_FSDP, TOK_DEV, KV)

        def add_group(total, pair):
            part = jnp.dot(pair[0].T, pair[1], preferred_element_type=jnp.float32)
            part = lax.optimization_barrier(part.astype(jnp.bfloat16))
            return (total + part.astype(jnp.float32), None)
        total, _ = lax.scan(add_group, jnp.zeros((D, KV), jnp.float32), (groups_n, groups_c))
        grad_normed = jnp.dot(cot, weight.T, preferred_element_type=jnp.float32)
        grad_normed = lax.optimization_barrier(grad_normed.astype(jnp.bfloat16)).astype(jnp.float32)
        scaled = grad_normed * norm_gain
        grad_in = inv * scaled - xfull * inv * inv * inv * lax.optimization_barrier(jnp.mean(xfull * scaled, axis=-1, keepdims=True))
        return (total.astype(jnp.bfloat16), grad_in.astype(jnp.bfloat16))
    grad_weight, grad_in = lax.map(replica, (per_rep, cot_rep, local_weight))
    grad_tokens = grad_in.reshape(TOKENS, D)
    anchor_full = anchor_weight.astype(jnp.float32)

    def add_delta(total, local):
        delta = anchor_full - local.astype(jnp.float32)
        codes, scale = quantize(delta)
        return (total + dequantize(codes, scale), None)
    summed, _ = lax.scan(add_delta, jnp.zeros((D, KV), jnp.float32), local_weight)
    pseudo = summed / N_REP
    new_moment = outer_mu * outer_moment + pseudo
    step = outer_rate * (pseudo + outer_mu * new_moment)
    new_master = outer_master - step
    codes, scale = quantize(step)
    synced_weight = (anchor_full - dequantize(codes, scale)).astype(jnp.bfloat16)
    return (grad_weight, grad_tokens, synced_weight, new_master, new_moment)
```

```python
import functools

import jax
import jax.numpy as jnp
from jax import lax
from jax.experimental import pallas as pl
from jax.experimental.pallas import tpu as pltpu
from jax.sharding import PartitionSpec as P

scale_eps = 1e-06
code_range = 448.0
norm_eps = 1e-05
outer_mu = 0.9
outer_rate = 0.7

SIDE = 4
ROWS = 32
F32 = jnp.float32
BF16 = jnp.bfloat16
PARAMS = pltpu.CompilerParams(vmem_limit_bytes=48 * 1024 * 1024)


def coords():
    index = lax.axis_index("fsdp")
    return index // SIDE, index % SIDE


def along_x(k):
    return [(x * SIDE + y, (x + k) % SIDE * SIDE + y) for x in range(SIDE) for y in range(SIDE)]


def along_y(k):
    return [(x * SIDE + y, x * SIDE + (y + k) % SIDE) for x in range(SIDE) for y in range(SIDE)]


def columns(step, width):
    return pl.ds(pl.multiple_of(step % SIDE * width, width), width)


def norm_kernel(tokens, gain, inv_out, *normed_out):
    x, _ = coords()
    width = normed_out[0].shape[1]
    full = tokens[...].astype(F32)
    inv = lax.rsqrt(jnp.mean(full * full, axis=-1, keepdims=True) + norm_eps)
    inv_out[...] = jnp.broadcast_to(inv, inv_out.shape)
    for k, out in enumerate(normed_out):
        cols = columns(x + k, width)
        out[...] = (tokens[:, cols].astype(F32) * inv * gain[:, cols]).astype(BF16)


def norm(tokens, gain):
    count, width = tokens.shape
    part = width // SIDE
    return pl.pallas_call(
        norm_kernel,
        grid=(count // ROWS,),
        in_specs=[pl.BlockSpec((ROWS, width), lambda i: (i, 0)), pl.BlockSpec((1, width), lambda i: (0, 0))],
        out_specs=[pl.BlockSpec((ROWS, 128), lambda i: (i, 0))]
        + [pl.BlockSpec((ROWS, part), lambda i: (i, 0))] * SIDE,
        out_shape=[jax.ShapeDtypeStruct((count, 128), F32)]
        + [jax.ShapeDtypeStruct((count, part), BF16)] * SIDE,
        compiler_params=PARAMS,
        cost_estimate=pl.CostEstimate(flops=4 * count * width, bytes_accessed=4 * count * width, transcendentals=0),
        name="norm",
    )(tokens, gain)


def back_kernel(*refs):
    cots, weights, outs = refs[:SIDE], refs[SIDE : 2 * SIDE], refs[2 * SIDE :]
    _, y = coords()
    rows = weights[0].shape[0]
    for j in range(SIDE):
        cols = columns(y - j + SIDE, rows)
        weight = weights[j][...]
        for k in range(SIDE):
            outs[k][:, cols] = lax.dot_general(
                cots[k][...], weight, (((1,), (1,)), ((), ())), preferred_element_type=F32
            ).astype(BF16)


def back(cots, weights):
    count, width = cots[0].shape
    rows = weights[0].shape[0]
    flops = 2 * SIDE * SIDE * count * rows * width
    return pl.pallas_call(
        back_kernel,
        out_shape=[jax.ShapeDtypeStruct((count, SIDE * rows), BF16)] * SIDE,
        compiler_params=PARAMS,
        cost_estimate=pl.CostEstimate(flops=flops, bytes_accessed=4 << 20, transcendentals=0),
        name="back",
    )(*cots, *weights)


def partial_kernel(*refs):
    normed, cots, outs = refs[:SIDE], refs[SIDE : 2 * SIDE], refs[2 * SIDE :]
    _, y = coords()
    rows = outs[0].shape[0]
    for j in range(SIDE):
        cols = columns(y + j, rows)
        total = jnp.zeros(outs[0].shape, F32)
        for k in range(SIDE):
            total = total + lax.dot_general(
                normed[k][:, cols], cots[k][...], (((0,), (0,)), ((), ())), preferred_element_type=F32
            )
        outs[j][...] = total.astype(outs[j].dtype)


def partial(normed, cots):
    count, width = cots[0].shape
    rows = normed[0].shape[1] // SIDE
    flops = 2 * SIDE * SIDE * count * rows * width
    return pl.pallas_call(
        partial_kernel,
        out_shape=[jax.ShapeDtypeStruct((rows, width), F32)]
        + [jax.ShapeDtypeStruct((rows, width), BF16)] * (SIDE - 1),
        compiler_params=PARAMS,
        cost_estimate=pl.CostEstimate(flops=flops, bytes_accessed=5 << 20, transcendentals=0),
        name="partial",
    )(*normed, *cots)


def finish_kernel(tokens, gain, inv_in, *refs):
    pieces, out = refs[:SIDE], refs[SIDE]
    x, _ = coords()
    width = pieces[0].shape[1]
    inv = inv_in[:, :1]
    total = jnp.zeros(inv.shape, F32)
    for k, piece in enumerate(pieces):
        cols = columns(x - k + SIDE, width)
        scaled = piece[...].astype(F32) * gain[:, cols]
        total = total + jnp.sum(tokens[:, cols].astype(F32) * scaled, axis=-1, keepdims=True)
    factor = inv * inv * inv * (total / (SIDE * width))
    for k, piece in enumerate(pieces):
        cols = columns(x - k + SIDE, width)
        scaled = piece[...].astype(F32) * gain[:, cols]
        out[:, cols] = (inv * scaled - tokens[:, cols].astype(F32) * factor).astype(BF16)


def finish(tokens, gain, inv, pieces):
    count, width = tokens.shape
    part = width // SIDE
    return pl.pallas_call(
        finish_kernel,
        grid=(count // ROWS,),
        in_specs=[
            pl.BlockSpec((ROWS, width), lambda i: (i, 0)),
            pl.BlockSpec((1, width), lambda i: (0, 0)),
            pl.BlockSpec((ROWS, 128), lambda i: (i, 0)),
        ]
        + [pl.BlockSpec((ROWS, part), lambda i: (i, 0))] * SIDE,
        out_specs=pl.BlockSpec((ROWS, width), lambda i: (i, 0)),
        out_shape=jax.ShapeDtypeStruct((count, width), BF16),
        compiler_params=PARAMS,
        cost_estimate=pl.CostEstimate(flops=6 * count * width, bytes_accessed=6 * count * width, transcendentals=0),
        name="finish",
    )(tokens, gain, inv, *pieces)


def requantized(values):
    parts = []
    for start in range(0, values.shape[-1], 128):
        block = values[..., start : start + 128]
        peak = jnp.max(jnp.abs(block), axis=-1, keepdims=True)
        scale = ((peak + scale_eps) / code_range).astype(BF16).astype(F32)
        parts.append((block / scale).astype(BF16).astype(F32) * scale)
    return jnp.concatenate(parts, axis=-1)


def outer_kernel(replicas, local, anchor, master, moment, master_out, moment_out, synced_out):
    slab = anchor.shape[0]
    start = anchor[...]
    total = jnp.zeros(start.shape, F32)
    held = local[...].astype(F32)
    for r in range(replicas):
        total = total + requantized(start - held[r * slab : (r + 1) * slab])
    pseudo = total / replicas
    new_moment = outer_mu * moment[...] + pseudo
    step = outer_rate * (pseudo + outer_mu * new_moment)
    moment_out[...] = new_moment
    master_out[...] = master[...] - step
    synced = start - requantized(step)
    synced_out[...] = jnp.concatenate([synced] * replicas, axis=0).astype(BF16)


def outer(local, anchor, master, moment, replicas):
    slab, width = master.shape
    return pl.pallas_call(
        functools.partial(outer_kernel, replicas),
        out_shape=[
            jax.ShapeDtypeStruct((slab, width), F32),
            jax.ShapeDtypeStruct((slab, width), F32),
            jax.ShapeDtypeStruct((slab * replicas, width), BF16),
        ],
        compiler_params=PARAMS,
        cost_estimate=pl.CostEstimate(
            flops=20 * replicas * slab * width, bytes_accessed=4 * replicas * slab * width, transcendentals=0
        ),
        name="outer",
    )(local, anchor, master, moment)


def local(tokens, cotangent, norm_gain, local_weight, anchor_weight, outer_master, outer_moment):
    key_width = cotangent.shape[1]
    weight = local_weight[0]
    own_rows = weight.shape[0]
    replicas = lax.axis_size("rep")
    slab = own_rows // replicas
    gain = norm_gain[None]

    def exchange(block):
        split = block.reshape(replicas, slab, key_width)
        return lax.all_to_all(split, "rep", split_axis=0, concat_axis=0, tiled=True).reshape(own_rows, key_width)

    gathered = exchange(weight)
    weights = [weight] + [lax.ppermute(weight, "fsdp", along_y(j)) for j in range(1, SIDE)]
    cots = [cotangent] + [lax.ppermute(cotangent, "fsdp", along_x(k)) for k in range(1, SIDE)]
    inv, *normed = norm(tokens, gain)
    normed = [normed[0]] + [lax.ppermute(normed[k], "fsdp", along_x(k)) for k in range(1, SIDE)]

    pieces = back([cots[(SIDE - k) % SIDE] for k in range(SIDE)], weights)
    pieces = [pieces[0]] + [lax.ppermute(pieces[k], "fsdp", along_x(k)) for k in range(1, SIDE)]

    parts = partial(normed, cots)
    grad_weight = parts[0]
    for j in range(1, SIDE):
        grad_weight = grad_weight + lax.ppermute(parts[j], "fsdp", along_y(j)).astype(F32)

    anchor_rows = lax.dynamic_slice_in_dim(anchor_weight, lax.axis_index("rep") * slab, slab, 0).astype(F32)
    new_master, new_moment, synced = outer(gathered, anchor_rows, outer_master, outer_moment, replicas)
    synced_weight = exchange(synced)

    grad_tokens = finish(tokens, gain, inv, pieces)
    return (grad_weight.astype(BF16)[None], grad_tokens, synced_weight, new_master, new_moment)


def solution(mesh):
    in_specs = (
        P(("rep", "fsdp"), None),
        P(("rep", "fsdp"), None),
        P(),
        P("rep", "fsdp", None),
        P("fsdp", None),
        P(("fsdp", "rep"), None),
        P(("fsdp", "rep"), None),
    )
    out_specs = (
        P("rep", "fsdp", None),
        P(("rep", "fsdp"), None),
        P("fsdp", None),
        P(("fsdp", "rep"), None),
        P(("fsdp", "rep"), None),
    )
    return jax.shard_map(local, mesh=mesh, in_specs=in_specs, out_specs=out_specs, check_vma=False)
```

```python
import functools

import jax
import jax.numpy as jnp
from jax import lax
from jax.experimental import pallas as pl
from jax.experimental.pallas import tpu as pltpu
from jax.sharding import PartitionSpec as P

scale_eps = 1e-06
code_range = 448.0
norm_eps = 1e-05
outer_mu = 0.9
outer_rate = 0.7

SIDE = 4
ROWS = 128
F32 = jnp.float32
BF16 = jnp.bfloat16
LARGE = pltpu.CompilerParams(vmem_limit_bytes=60 * 1024 * 1024)
PARAMS = pltpu.CompilerParams(vmem_limit_bytes=30 * 1024 * 1024)
COST = pl.CostEstimate(flops=1, bytes_accessed=1, transcendentals=0)


def coords():
    index = lax.axis_index("fsdp")
    return index // SIDE, index % SIDE


def along_x(k):
    return [(x * SIDE + y, (x + k) % SIDE * SIDE + y) for x in range(SIDE) for y in range(SIDE)]


def along_y(k):
    return [(x * SIDE + y, x * SIDE + (y + k) % SIDE) for x in range(SIDE) for y in range(SIDE)]


def columns(step, width):
    return pl.ds(pl.multiple_of(step % SIDE * width, width), width)


def norm_kernel(tokens, cotangent, gain, inv_out, own_out, *packs):
    x, _ = coords()
    width = own_out.shape[1]
    full = tokens[...].astype(F32)
    inv = lax.rsqrt(jnp.mean(full * full, axis=-1, keepdims=True) + norm_eps)
    inv_out[...] = jnp.broadcast_to(inv, inv_out.shape)
    for k, out in enumerate((own_out,) + packs):
        cols = columns(x + k, width)
        out[:, :width] = (tokens[:, cols].astype(F32) * inv * gain[:, cols]).astype(BF16)
    for pack in packs:
        pack[:, width:] = cotangent[...]


def norm(tokens, cotangent, gain):
    count, width = tokens.shape
    part, keys = width // SIDE, cotangent.shape[1]

    def rows_of(columns):
        return pl.BlockSpec((ROWS, columns), lambda i: (i, 0))

    return pl.pallas_call(
        norm_kernel,
        grid=(count // ROWS,),
        in_specs=[rows_of(width), rows_of(keys), pl.BlockSpec((1, width), lambda i: (0, 0))],
        out_specs=[rows_of(128), rows_of(part)] + [rows_of(part + keys)] * (SIDE - 1),
        out_shape=[jax.ShapeDtypeStruct((count, 128), F32), jax.ShapeDtypeStruct((count, part), BF16)]
        + [jax.ShapeDtypeStruct((count, part + keys), BF16)] * (SIDE - 1),
        compiler_params=LARGE,
        cost_estimate=COST,
        name="norm",
    )(tokens, cotangent, gain)


def keys_of(source, width):
    place = source.shape[1] // width - 1
    return pl.BlockSpec((source.shape[0], width), lambda i: (0, place))


def back_kernel(number, *refs):
    cots, weight, outs = refs[:number], refs[number], refs[number + 1 :]
    for cot, out in zip(cots, outs, strict=True):
        out[...] = lax.dot_general(
            cot[...], weight[...], (((1,), (1,)), ((), ())), preferred_element_type=F32
        ).astype(BF16)


def back(sources, weight):
    count = sources[0].shape[0]
    rows, width = weight.shape
    number, block = len(sources), rows // 2
    return pl.pallas_call(
        functools.partial(back_kernel, number),
        grid=(rows // block,),
        in_specs=[keys_of(source, width) for source in sources]
        + [pl.BlockSpec((block, width), lambda i: (i, 0))],
        out_specs=[pl.BlockSpec((count, block), lambda i: (0, i))] * number,
        out_shape=[jax.ShapeDtypeStruct((count, rows), BF16)] * number,
        compiler_params=PARAMS,
        cost_estimate=COST,
        name="back",
    )(*sources, weight)


def normed_of(source, rows):
    return pl.BlockSpec((source.shape[0], rows), lambda j: (0, j))


def partial_kernel(number, *refs):
    normed, cots, out = refs[:number], refs[number : 2 * number], refs[-1]
    total = jnp.zeros(out.shape, F32)
    for block, cot in zip(normed, cots, strict=True):
        total = total + lax.dot_general(
            block[...], cot[...], (((0,), (0,)), ((), ())), preferred_element_type=F32
        )
    out[...] = total.astype(BF16)


def partial(own, cotangent, packs):
    width = cotangent.shape[1]
    rows = own.shape[1] // 2
    return pl.pallas_call(
        functools.partial(partial_kernel, len(packs) + 1),
        grid=(2,),
        in_specs=[normed_of(source, rows) for source in (own, *packs)]
        + [keys_of(source, width) for source in (cotangent, *packs)],
        out_specs=pl.BlockSpec((rows, width), lambda j: (j, 0)),
        out_shape=jax.ShapeDtypeStruct((own.shape[1], width), BF16),
        compiler_params=PARAMS,
        cost_estimate=COST,
        name="partial",
    )(own, *packs, cotangent, *packs)


def finish_kernel(tokens, gain, inv_in, *refs):
    pieces, out = refs[:SIDE], refs[SIDE]
    x, _ = coords()
    width = pieces[0].shape[1]
    inv = inv_in[:, :1]
    total = jnp.zeros(inv.shape, F32)
    for k, piece in zip((2, 1, 3, 0), pieces, strict=True):
        cols = columns(x - k + SIDE, width)
        scaled = piece[...].astype(F32) * gain[:, cols]
        total = total + jnp.sum(tokens[:, cols].astype(F32) * scaled, axis=-1, keepdims=True)
    factor = inv * inv * inv * (total / (SIDE * width))
    for k, piece in zip((2, 1, 3, 0), pieces, strict=True):
        cols = columns(x - k + SIDE, width)
        scaled = piece[...].astype(F32) * gain[:, cols]
        out[:, cols] = (inv * scaled - tokens[:, cols].astype(F32) * factor).astype(BF16)


def finish(tokens, gain, inv, pieces):
    count, width = tokens.shape
    part = width // SIDE
    return pl.pallas_call(
        finish_kernel,
        grid=(count // ROWS,),
        in_specs=[
            pl.BlockSpec((ROWS, width), lambda i: (i, 0)),
            pl.BlockSpec((1, width), lambda i: (0, 0)),
            pl.BlockSpec((ROWS, 128), lambda i: (i, 0)),
        ]
        + [pl.BlockSpec((ROWS, part), lambda i: (i, 0))] * SIDE,
        out_specs=pl.BlockSpec((ROWS, width), lambda i: (i, 0)),
        out_shape=jax.ShapeDtypeStruct((count, width), BF16),
        compiler_params=LARGE,
        cost_estimate=COST,
        name="finish",
    )(tokens, gain, inv, *pieces)


def requantized(values):
    parts = []
    for start in range(0, values.shape[-1], 128):
        block = values[..., start : start + 128]
        peak = jnp.max(jnp.abs(block), axis=-1, keepdims=True)
        scale = ((peak + scale_eps) / code_range).astype(BF16).astype(F32)
        parts.append((block / scale).astype(BF16).astype(F32) * scale)
    return jnp.concatenate(parts, axis=-1)


def outer_kernel(local, anchor, master, moment, master_out, moment_out, synced_out):
    slab = master.shape[0]
    replicas = local.shape[0] // slab
    pair = anchor[...].astype(F32)
    start = jnp.where(lax.axis_index("rep") % 2 == 0, pair[:slab], pair[slab:])
    total = jnp.zeros(start.shape, F32)
    held = local[...].astype(F32)
    for r in range(replicas):
        total = total + requantized(start - held[r * slab : (r + 1) * slab])
    pseudo = total / replicas
    new_moment = outer_mu * moment[...] + pseudo
    step = outer_rate * (pseudo + outer_mu * new_moment)
    moment_out[...] = new_moment
    master_out[...] = master[...] - step
    synced = start - requantized(step)
    synced_out[...] = jnp.concatenate([synced] * replicas, axis=0).astype(BF16)


def outer(local, anchor, master, moment):
    slab, width = master.shape
    own = pl.BlockSpec((slab, width), lambda i: (0, 0))
    whole = pl.BlockSpec(local.shape, lambda i: (0, 0))
    return pl.pallas_call(
        outer_kernel,
        grid=(1,),
        in_specs=[whole, pl.BlockSpec((2 * slab, width), lambda i: (lax.axis_index("rep") // 2, 0)), own, own],
        out_specs=[own, own, whole],
        out_shape=[
            jax.ShapeDtypeStruct((slab, width), F32),
            jax.ShapeDtypeStruct((slab, width), F32),
            jax.ShapeDtypeStruct(local.shape, BF16),
        ],
        compiler_params=PARAMS,
        cost_estimate=COST,
        name="outer",
    )(local, anchor, master, moment)


def local(tokens, cotangent, norm_gain, local_weight, anchor_weight, outer_master, outer_moment):
    key_width = cotangent.shape[1]
    weight = local_weight[0]
    own_rows = weight.shape[0]
    replicas = lax.axis_size("rep")
    slab = own_rows // replicas
    gain = norm_gain[None]

    def exchange(block):
        split = block.reshape(replicas, slab, key_width)
        return lax.all_to_all(split, "rep", split_axis=0, concat_axis=0, tiled=True).reshape(own_rows, key_width)

    line = [[x * SIDE + y for y in range(SIDE)] for x in range(SIDE)]
    weights = lax.all_gather(weight, "fsdp", axis=0, tiled=True, axis_index_groups=line)
    inv, own, *packs = norm(tokens, cotangent, gain)
    second = lax.ppermute(packs[1], "fsdp", along_x(2))
    packs = [lax.ppermute(packs[0], "fsdp", along_x(1)), second, lax.ppermute(packs[2], "fsdp", along_x(3))]
    gathered = exchange(weight)
    new_master, new_moment, synced = outer(gathered, anchor_weight, outer_master, outer_moment)

    own, _ = lax.optimization_barrier((own, synced))
    part = partial(own, cotangent, [packs[1], packs[0], packs[2]])
    grad_weight = lax.psum_scatter(part, "fsdp", scatter_dimension=0, tiled=True, axis_index_groups=line)

    weights, _ = lax.optimization_barrier((weights, part))
    across, ahead, behind, kept = back([packs[1], packs[2], packs[0], cotangent], weights)
    across = lax.ppermute(across, "fsdp", along_x(2))
    pieces = [across, lax.ppermute(ahead, "fsdp", along_x(1)), lax.ppermute(behind, "fsdp", along_x(3)), kept]

    synced, _ = lax.optimization_barrier((synced, kept))
    synced_weight = exchange(synced)
    grad_tokens = finish(tokens, gain, inv, pieces)
    synced_weight, grad_tokens = lax.optimization_barrier((synced_weight, grad_tokens))
    return (grad_weight[None], grad_tokens, synced_weight, new_master, new_moment)


def solution(mesh):
    in_specs = (
        P(("rep", "fsdp"), None),
        P(("rep", "fsdp"), None),
        P(),
        P("rep", "fsdp", None),
        P("fsdp", None),
        P(("fsdp", "rep"), None),
        P(("fsdp", "rep"), None),
    )
    out_specs = (
        P("rep", "fsdp", None),
        P(("rep", "fsdp"), None),
        P("fsdp", None),
        P(("fsdp", "rep"), None),
        P(("fsdp", "rep"), None),
    )
    return jax.shard_map(local, mesh=mesh, in_specs=in_specs, out_specs=out_specs, check_vma=False)
```

```python
import functools

import jax
import jax.numpy as jnp
from jax import lax
from jax.experimental import pallas as pl
from jax.experimental.pallas import tpu as pltpu
from jax.sharding import PartitionSpec as P

scale_eps = 1e-06
code_range = 448.0
norm_eps = 1e-05
outer_mu = 0.9
outer_rate = 0.7

SIDE = 4
ROWS = 128
F32 = jnp.float32
BF16 = jnp.bfloat16
LARGE = pltpu.CompilerParams(vmem_limit_bytes=60 * 1024 * 1024)
PARAMS = pltpu.CompilerParams(vmem_limit_bytes=30 * 1024 * 1024)
COST = pl.CostEstimate(flops=1, bytes_accessed=1, transcendentals=0)
MIDDLE = pl.CostEstimate(flops=2 << 30, bytes_accessed=1, transcendentals=0)
LONG = pl.CostEstimate(flops=1 << 35, bytes_accessed=1 << 28, transcendentals=0)


def coords():
    index = lax.axis_index("fsdp")
    return index // SIDE, index % SIDE


def along_x(k):
    return [(x * SIDE + y, (x + k) % SIDE * SIDE + y) for x in range(SIDE) for y in range(SIDE)]


def along_y(k):
    return [(x * SIDE + y, x * SIDE + (y + k) % SIDE) for x in range(SIDE) for y in range(SIDE)]


def columns(step, width):
    return pl.ds(pl.multiple_of(step % SIDE * width, width), width)


def norm_kernel(tokens, cotangent, gain, inv_out, own_out, *packs):
    x, _ = coords()
    width = own_out.shape[1]
    full = tokens[...].astype(F32)
    inv = lax.rsqrt(jnp.mean(full * full, axis=-1, keepdims=True) + norm_eps)
    inv_out[...] = jnp.broadcast_to(inv, inv_out.shape)
    for k, out in enumerate((own_out,) + packs):
        cols = columns(x + k, width)
        out[:, :width] = (tokens[:, cols].astype(F32) * inv * gain[:, cols]).astype(BF16)
    for pack in packs:
        pack[:, width:] = cotangent[...]


def norm(tokens, cotangent, gain):
    count, width = tokens.shape
    part, keys = width // SIDE, cotangent.shape[1]

    def rows_of(columns):
        return pl.BlockSpec((ROWS, columns), lambda i: (i, 0))

    return pl.pallas_call(
        norm_kernel,
        grid=(count // ROWS,),
        in_specs=[rows_of(width), rows_of(keys), pl.BlockSpec((1, width), lambda i: (0, 0))],
        out_specs=[rows_of(128), rows_of(part)] + [rows_of(part + keys)] * (SIDE - 1),
        out_shape=[jax.ShapeDtypeStruct((count, 128), F32), jax.ShapeDtypeStruct((count, part), BF16)]
        + [jax.ShapeDtypeStruct((count, part + keys), BF16)] * (SIDE - 1),
        compiler_params=LARGE,
        cost_estimate=COST,
        name="norm",
    )(tokens, cotangent, gain)


def keys_of(source, width):
    place = source.shape[1] // width - 1
    return pl.BlockSpec((source.shape[0], width), lambda i: (0, place))


def back_kernel(number, *refs):
    cots, weight, outs = refs[:number], refs[number], refs[number + 1 :]
    for cot, out in zip(cots, outs, strict=True):
        out[...] = lax.dot_general(
            cot[...], weight[...], (((1,), (1,)), ((), ())), preferred_element_type=F32
        ).astype(BF16)


def back(sources, weight):
    count = sources[0].shape[0]
    rows, width = weight.shape
    number, block = len(sources), rows // 2
    return pl.pallas_call(
        functools.partial(back_kernel, number),
        grid=(rows // block,),
        in_specs=[keys_of(source, width) for source in sources]
        + [pl.BlockSpec((block, width), lambda i: (i, 0))],
        out_specs=[pl.BlockSpec((count, block), lambda i: (0, i))] * number,
        out_shape=[jax.ShapeDtypeStruct((count, rows), BF16)] * number,
        compiler_params=PARAMS,
        cost_estimate=COST,
        name="back",
    )(*sources, weight)


def normed_of(source, rows):
    return pl.BlockSpec((source.shape[0], rows), lambda j: (0, j))


def partial_kernel(number, *refs):
    normed, cots, out = refs[:number], refs[number : 2 * number], refs[-1]
    total = jnp.zeros(out.shape, F32)
    for block, cot in zip(normed, cots, strict=True):
        total = total + lax.dot_general(
            block[...], cot[...], (((0,), (0,)), ((), ())), preferred_element_type=F32
        )
    out[...] = total.astype(BF16)


def partial(own, cotangent, packs):
    width = cotangent.shape[1]
    rows = own.shape[1] // 2
    return pl.pallas_call(
        functools.partial(partial_kernel, len(packs) + 1),
        grid=(2,),
        in_specs=[normed_of(source, rows) for source in (own, *packs)]
        + [keys_of(source, width) for source in (cotangent, *packs)],
        out_specs=pl.BlockSpec((rows, width), lambda j: (j, 0)),
        out_shape=jax.ShapeDtypeStruct((own.shape[1], width), BF16),
        compiler_params=PARAMS,
        cost_estimate=COST,
        name="partial",
    )(own, *packs, cotangent, *packs)


def finish_kernel(tokens, gain, inv_in, *refs):
    pieces, out = refs[:SIDE], refs[SIDE]
    x, _ = coords()
    width = pieces[0].shape[1]
    inv = inv_in[:, :1]
    total = jnp.zeros(inv.shape, F32)
    for k, piece in zip((2, 1, 3, 0), pieces, strict=True):
        cols = columns(x - k + SIDE, width)
        scaled = piece[...].astype(F32) * gain[:, cols]
        total = total + jnp.sum(tokens[:, cols].astype(F32) * scaled, axis=-1, keepdims=True)
    factor = inv * inv * inv * (total / (SIDE * width))
    for k, piece in zip((2, 1, 3, 0), pieces, strict=True):
        cols = columns(x - k + SIDE, width)
        scaled = piece[...].astype(F32) * gain[:, cols]
        out[:, cols] = (inv * scaled - tokens[:, cols].astype(F32) * factor).astype(BF16)


def finish(tokens, gain, inv, pieces):
    count, width = tokens.shape
    part = width // SIDE
    return pl.pallas_call(
        finish_kernel,
        grid=(count // ROWS,),
        in_specs=[
            pl.BlockSpec((ROWS, width), lambda i: (i, 0)),
            pl.BlockSpec((1, width), lambda i: (0, 0)),
            pl.BlockSpec((ROWS, 128), lambda i: (i, 0)),
        ]
        + [pl.BlockSpec((ROWS, part), lambda i: (i, 0))] * SIDE,
        out_specs=pl.BlockSpec((ROWS, width), lambda i: (i, 0)),
        out_shape=jax.ShapeDtypeStruct((count, width), BF16),
        compiler_params=LARGE,
        cost_estimate=COST,
        name="finish",
    )(tokens, gain, inv, *pieces)


def requantized(values):
    parts = []
    for start in range(0, values.shape[-1], 128):
        block = values[..., start : start + 128]
        peak = jnp.max(jnp.abs(block), axis=-1, keepdims=True)
        scale = ((peak + scale_eps) / code_range).astype(BF16).astype(F32)
        parts.append((block / scale).astype(BF16).astype(F32) * scale)
    return jnp.concatenate(parts, axis=-1)


def outer_kernel(local, anchor, master, moment, master_out, moment_out, synced_out):
    slab = master.shape[0]
    replicas = local.shape[0] // slab
    pair = anchor[...].astype(F32)
    start = jnp.where(lax.axis_index("rep") % 2 == 0, pair[:slab], pair[slab:])
    total = jnp.zeros(start.shape, F32)
    held = local[...].astype(F32)
    for r in range(replicas):
        total = total + requantized(start - held[r * slab : (r + 1) * slab])
    pseudo = total / replicas
    new_moment = outer_mu * moment[...] + pseudo
    step = outer_rate * (pseudo + outer_mu * new_moment)
    moment_out[...] = new_moment
    master_out[...] = master[...] - step
    synced = start - requantized(step)
    synced_out[...] = jnp.concatenate([synced] * replicas, axis=0).astype(BF16)


def outer(local, anchor, master, moment):
    slab, width = master.shape
    own = pl.BlockSpec((slab, width), lambda i: (0, 0))
    whole = pl.BlockSpec(local.shape, lambda i: (0, 0))
    return pl.pallas_call(
        outer_kernel,
        grid=(1,),
        in_specs=[whole, pl.BlockSpec((2 * slab, width), lambda i: (lax.axis_index("rep") // 2, 0)), own, own],
        out_specs=[own, own, whole],
        out_shape=[
            jax.ShapeDtypeStruct((slab, width), F32),
            jax.ShapeDtypeStruct((slab, width), F32),
            jax.ShapeDtypeStruct(local.shape, BF16),
        ],
        compiler_params=PARAMS,
        cost_estimate=MIDDLE,
        name="outer",
    )(local, anchor, master, moment)


def place_kernel(block, out):
    out[...] = block[...]


def place(block):
    return pl.pallas_call(
        place_kernel,
        out_shape=jax.ShapeDtypeStruct(block.shape, block.dtype),
        compiler_params=PARAMS,
        cost_estimate=LONG,
        name="place",
    )(block)


def local(tokens, cotangent, norm_gain, local_weight, anchor_weight, outer_master, outer_moment):
    key_width = cotangent.shape[1]
    weight = local_weight[0]
    own_rows = weight.shape[0]
    replicas = lax.axis_size("rep")
    slab = own_rows // replicas
    gain = norm_gain[None]

    def exchange(block):
        split = block.reshape(replicas, slab, key_width)
        return lax.all_to_all(split, "rep", split_axis=0, concat_axis=0, tiled=True).reshape(own_rows, key_width)

    line = [[x * SIDE + y for y in range(SIDE)] for x in range(SIDE)]
    weights = lax.all_gather(weight, "fsdp", axis=0, tiled=True, axis_index_groups=line)
    inv, own, *packs = norm(tokens, cotangent, gain)
    second = lax.ppermute(packs[1], "fsdp", along_x(2))
    packs = [lax.ppermute(packs[0], "fsdp", along_x(1)), second, lax.ppermute(packs[2], "fsdp", along_x(3))]
    gathered = exchange(weight)
    gathered, packs[1] = lax.optimization_barrier((gathered, packs[1]))
    new_master, new_moment, synced = outer(gathered, anchor_weight, outer_master, outer_moment)
    synced_weight = place(exchange(synced))

    own, _ = lax.optimization_barrier((own, synced))
    part = partial(own, cotangent, [packs[1], packs[0], packs[2]])
    grad_weight = lax.psum_scatter(part, "fsdp", scatter_dimension=0, tiled=True, axis_index_groups=line)
    weights, _ = lax.optimization_barrier((weights, part))
    across, ahead, behind, kept = back([packs[1], packs[2], packs[0], cotangent], weights)
    across = lax.ppermute(across, "fsdp", along_x(2))
    pieces = [across, lax.ppermute(ahead, "fsdp", along_x(1)), lax.ppermute(behind, "fsdp", along_x(3)), kept]
    inv, synced_weight = lax.optimization_barrier((inv, synced_weight))
    grad_tokens = finish(tokens, gain, inv, pieces)
    return (grad_weight[None], grad_tokens, synced_weight, new_master, new_moment)


def solution(mesh):
    in_specs = (
        P(("rep", "fsdp"), None),
        P(("rep", "fsdp"), None),
        P(),
        P("rep", "fsdp", None),
        P("fsdp", None),
        P(("fsdp", "rep"), None),
        P(("fsdp", "rep"), None),
    )
    out_specs = (
        P("rep", "fsdp", None),
        P(("rep", "fsdp"), None),
        P("fsdp", None),
        P(("fsdp", "rep"), None),
        P(("fsdp", "rep"), None),
    )
    return jax.shard_map(local, mesh=mesh, in_specs=in_specs, out_specs=out_specs, check_vma=False)
```
